256 devices in a mesh: gx: 8 (over y, core), gy: 4 (over x), gz: 8 (over z).
Axes of the slice: x: 4, y: 4, z: 8, core: 2. Of those that a mesh axis runs over, the one named last changes fastest.
Arguments:
- positions: float32 [8, 4, 8, 128, 3], P('gx', 'gy', 'gz'), may hold values from 0 to 1
- species: int32 [8, 4, 8, 128], P('gx', 'gy', 'gz'), may hold values from 0 to 4
- send_list: int32 [8, 4, 8, 27, 8], P('gx', 'gy', 'gz'), may hold values from -1 to 127, as said below
- pair_first: int32 [8, 4, 8, 2048], P('gx', 'gy', 'gz'), may hold values from 0 to 127, as said below
- pair_second: int32 [8, 4, 8, 2048], P('gx', 'gy', 'gz'), may hold values from -1 to 337, as said below
- species_embed: float32 [5, 64], replicated, may hold values from -6 to 6
- w_latent: bfloat16 [136, 256], replicated, may hold values from -2 to 2
- w_channel: bfloat16 [256, 192], replicated, may hold values from -0.375 to 0.375
- w_energy: bfloat16 [256, 128], replicated, may hold values from -0.375 to 0.375
- w_invariant: bfloat16 [192, 128], replicated, may hold values from -0.4375 to 0.4375
- energy_vector: float32 [128], replicated, may hold values from -0.5 to 0.5
Outputs:
- forces: float32 [8, 4, 8, 128, 3], P('gx', 'gy', 'gz')
- energy: float32 [1], replicated
The draws below stay inside these ranges and needn't reach their ends.
Inputs may be any that keep to these rules, and one draw needn't show every extreme that they name: `send_list`: row s = 9a + 3b + c of a device's list names distinct owned atoms whose copies go to the device at offset (a - 1, b - 1, c - 1); used entries come first, -1 fills the rest; row 13 is all -1; every row other than 13 uses at least one entry; every device has a full row (8 entries) in every draw. `pair_first`: an owned atom; 0 where pair_second is -1. `pair_second`: -1 marks padding and follows all used entries of a device. A used entry is an owned atom other than the pair's first one, or the row 128 + s * 8 + k of block s whose column k the sending device fills. Some device uses all 2048 entries in every draw, and some entry reaches the largest value in every draw.
All inputs are finite; a program needn't handle non-finite values.
Results may differ from the reference program's by a relative error of at most 0.012.
The reference program's roundings to bfloat16 on the way count: a program that leaves them out, or rounds other values in their place, can miss the bound.
Values sent between devices are 32-bit elements; how exact they have to be, the bound alone decides.
No kernel may reach another device: no remote copies, remote signals or barrier semaphores. Data moves between devices by JAX's collectives and lax.ppermute only.
A program may use at most 64 MiB of HBM per device.

```python
import math
import jax
import jax.numpy as jnp
import numpy as np
from jax import lax

ATOM_DEV = 128
GHOSTS = 8
PAIRS_DEV = 2048
C = 64
HID = 256
HID2 = 128
NB = 8
NSPEC = 5
N_GX = 8
N_GY = 4
N_GZ = 8


FACE_SLOTS = np.array([4, 10, 12, 14, 16, 22])


SLOT_KIND = np.array([int(slot_index // 9 != 1) + int(slot_index // 3 % 3 != 1) + int(slot_index % 3 != 1) for slot_index in range(27)])


def feeder_device(key):
    return jax.random.randint(jax.random.fold_in(key, 303), (), 0, N_GX * N_GY * N_GZ)


def ghost_counts(key):
    feeder = feeder_device(key)
    key = jax.random.fold_in(key, 101)
    subkeys = jax.random.split(key, 4)
    grid_shape = (N_GX, N_GY, N_GZ, 27)
    face_count = GHOSTS - jax.random.randint(subkeys[0], grid_shape, 0, GHOSTS // 4 + 1)
    edge_count = jax.random.randint(subkeys[1], grid_shape, GHOSTS // 4, GHOSTS // 2 + 1)
    corner = jax.random.randint(subkeys[2], grid_shape, 1, GHOSTS // 8 + 2)
    slot_kind = jnp.asarray(SLOT_KIND)
    counts = jnp.where(slot_kind == 1, face_count, jnp.where(slot_kind == 2, edge_count, jnp.where(slot_kind == 3, corner, 0)))
    chosen = jax.random.randint(subkeys[3], (N_GX, N_GY, N_GZ, 1), 0, 6)
    full_slot = jnp.asarray(FACE_SLOTS)[chosen]
    counts = jnp.where(jnp.arange(27) == full_slot, GHOSTS, counts)
    flat_device = jnp.arange(N_GX * N_GY * N_GZ).reshape(N_GX, N_GY, N_GZ, 1)
    corner_full = jnp.logical_and(flat_device == feeder, jnp.arange(27) == 0)
    counts = jnp.where(corner_full, GHOSTS // 8 + 1, counts)
    return counts.astype(jnp.int32)


def received_counts(counts):
    columns = []
    for slot_index in range(27):
        roll_shift = (1 - slot_index // 9, 1 - slot_index // 3 % 3, 1 - slot_index % 3)
        columns.append(jnp.roll(counts[..., 26 - slot_index], roll_shift, axis=(0, 1, 2)))
    return jnp.stack(columns, axis=-1)


def pair_table(key):
    counts = received_counts(ghost_counts(key))
    feeder = feeder_device(key)
    feed_x = feeder // (N_GY * N_GZ)
    feed_y = feeder // N_GZ % N_GY
    feed_z = feeder % N_GZ
    fullest = ((feed_x - 1) % N_GX * N_GY + (feed_y - 1) % N_GY) * N_GZ + (feed_z - 1) % N_GZ
    key = jax.random.fold_in(key, 202)
    subkeys = jax.random.split(key, 7)
    pair_shape = (N_GX, N_GY, N_GZ, PAIRS_DEV)
    first_atom = jax.random.randint(subkeys[0], pair_shape, 0, ATOM_DEV)
    other_atom = jax.random.randint(subkeys[1], pair_shape, 0, ATOM_DEV - 1)
    other_atom = other_atom + (other_atom >= first_atom).astype(jnp.int32)
    slot_pick = jax.random.randint(subkeys[2], pair_shape, 0, 26)
    slot_index = slot_pick + (slot_pick >= 13).astype(jnp.int32)
    slot_count = jnp.take_along_axis(counts, slot_index, axis=-1)
    entry_index = jax.random.randint(subkeys[3], pair_shape, 0, 2 ** 20) % slot_count
    ghost_row = ATOM_DEV + slot_index * GHOSTS + entry_index
    use_ghost = jax.random.randint(subkeys[4], pair_shape, 0, 2) == 1
    second_atom = jnp.where(use_ghost, ghost_row, other_atom)
    used_count = PAIRS_DEV - jax.random.randint(subkeys[5], (N_GX, N_GY, N_GZ, 1), 0, PAIRS_DEV * 11 // 20 + 1)
    flat_device = jnp.arange(N_GX * N_GY * N_GZ).reshape(N_GX, N_GY, N_GZ, 1)
    used_count = jnp.where(flat_device == fullest, PAIRS_DEV, used_count)
    top_entry = jnp.logical_and(flat_device == fullest, jnp.arange(PAIRS_DEV) == PAIRS_DEV - 1)
    second_atom = jnp.where(top_entry, ATOM_DEV + 26 * GHOSTS + GHOSTS // 8, second_atom)
    live_mask = jnp.arange(PAIRS_DEV) < used_count
    return (jnp.where(live_mask, first_atom, 0).astype(jnp.int32), jnp.where(live_mask, second_atom, -1).astype(jnp.int32))


def draw_send_list(key, part):
    counts = ghost_counts(key)
    key = jax.random.fold_in(key, 1)
    scores = jax.random.randint(key, (N_GX, N_GY, N_GZ, 27, ATOM_DEV), 0, 2 ** 14) * ATOM_DEV + jnp.arange(ATOM_DEV)
    ordering = jnp.argsort(scores, axis=-1)[..., :GHOSTS].astype(jnp.int32)
    return jnp.where(jnp.arange(GHOSTS) < counts[..., None], ordering, -1).astype(jnp.int32)


def draw_pair_first(key, part):
    first_atom, second_atom = pair_table(key)
    key = jax.random.fold_in(key, 2)
    return first_atom


def draw_pair_second(key, part):
    first_atom, second_atom = pair_table(key)
    key = jax.random.fold_in(key, 3)
    return second_atom


def draw_w_latent(key, part):
    key = jax.random.fold_in(key, 4)
    radial_key, embed_key = jax.random.split(key)
    plain_scale = (NB + 2 * C) ** (-0.5)
    radial = jnp.clip(0.7 * jax.random.normal(radial_key, (NB, HID), jnp.float32), -2.0, 2.0)
    rest = jnp.clip(plain_scale * jax.random.normal(embed_key, (2 * C, HID), jnp.float32), -6.0 * plain_scale, 6.0 * plain_scale)
    return jnp.concatenate([radial, rest], axis=0).astype(jnp.bfloat16)


def with_ends(entries, key, least, top_value):
    dims = entries.shape
    index_at = [jax.random.randint(jax.random.fold_in(key, axis), (), 0, dims[axis]) for axis in range(len(dims))]
    entries = entries.at[tuple(index_at)].set(least)
    longest = dims.index(max(dims))
    index_at[longest] = (index_at[longest] + 1) % dims[longest]
    return entries.at[tuple(index_at)].set(top_value)


def steps_of(stream_key, shape, cuts, least, high):
    def one(position, blocks):
        steps = jax.random.uniform(jax.random.fold_in(jax.random.fold_in(stream_key, 6), position), (blocks,), jnp.float32, least / len(cuts), high / len(cuts))
        return jnp.repeat(jnp.exp(steps), shape[position] // blocks).reshape((-1,) + (1,) * (len(shape) - position - 1))

    level = one(*cuts[0])
    for cut in cuts[1:]:
        level = level * one(*cut)
    return level


def bell_draw(rng, extent, scale, bound, kind=jnp.bfloat16):
    drawn = scale * jax.random.normal(rng, extent, jnp.float32)
    return jnp.clip(drawn, min=-bound, max=bound).astype(kind)


def setup_inputs(seed: int = 0) -> dict:
    streams_of = jax.random.split(jax.random.key(seed), 12)
    positions = jnp.clip(1.0 * jax.random.uniform(streams_of[0], (N_GX, N_GY, N_GZ, ATOM_DEV, 3), jnp.float32) ** steps_of(streams_of[0], (N_GX, N_GY, N_GZ, ATOM_DEV, 3), ((0, 8), (1, 4), (2, 8)), -0.2, 0.2), 0.0, 1.0)
    species = with_ends(jax.random.randint(streams_of[1], (N_GX, N_GY, N_GZ, ATOM_DEV), 0, NSPEC), jax.random.fold_in(streams_of[1], 1), 0, NSPEC - 1).astype(jnp.int32)
    send_list = draw_send_list(jax.random.fold_in(streams_of[11], 71), 0)
    pair_first = draw_pair_first(jax.random.fold_in(streams_of[11], 71), 0)
    pair_second = draw_pair_second(jax.random.fold_in(streams_of[11], 71), 0)
    species_embed = bell_draw(streams_of[5], (NSPEC, C), 1.0, 6.0, jnp.float32)
    w_latent = draw_w_latent(jax.random.fold_in(streams_of[11], 71), 0)
    w_channel = bell_draw(streams_of[7], (HID, 3 * C), HID ** -0.5, 0.375)
    w_energy = bell_draw(streams_of[8], (HID, HID2), HID ** -0.5, 0.375)
    w_invariant = bell_draw(streams_of[9], (3 * C, HID2), (3 * C) ** -0.5, 0.4375)
    energy_vector = bell_draw(streams_of[10], (HID2,), HID2 ** -0.5, 0.5, jnp.float32)
    return {"positions": positions, "species": species, "send_list": send_list, "pair_first": pair_first, "pair_second": pair_second, "species_embed": species_embed, "w_latent": w_latent, "w_channel": w_channel, "w_energy": w_energy, "w_invariant": w_invariant, "energy_vector": energy_vector}


DEGREE = np.array([0, 1, 1, 1, 2, 2, 2, 2, 2])
PARITY = np.array([1.0, -1.0, -1.0, -1.0, 1.0, 1.0, 1.0, 1.0, 1.0], dtype=np.float32)
ENV_SCALE = 0.1
RADIAL_STEP = 0.5
RADIAL_WIDTH = 0.35
ROOT_THREE = math.sqrt(3.0)
ROOT_FIVE = math.sqrt(5.0)
ROOT_FIFTEEN = math.sqrt(15.0)

def harmonics(displace):
    coord_x = displace[:, 0]
    coord_y = displace[:, 1]
    coord_z = displace[:, 2]
    radius_sq = coord_x * coord_x + coord_y * coord_y + coord_z * coord_z
    return jnp.stack([jnp.ones_like(coord_x), ROOT_THREE * coord_x, ROOT_THREE * coord_y, ROOT_THREE * coord_z, ROOT_FIFTEEN * coord_x * coord_y, ROOT_FIFTEEN * coord_y * coord_z, 0.5 * ROOT_FIVE * (3.0 * coord_z * coord_z - radius_sq), ROOT_FIFTEEN * coord_x * coord_z, 0.5 * ROOT_FIFTEEN * (coord_x * coord_x - coord_y * coord_y)], axis=1)

def pair_latent(displace, onehot_first, onehot_second, species_embed, w_latent, w_channel):
    radius_sq = lax.optimization_barrier(jnp.sum(displace * displace, axis=1))
    basis_count = w_latent.shape[0] - 2 * species_embed.shape[1]
    centres = RADIAL_STEP * jnp.arange(basis_count).astype(displace.dtype)
    radial = jnp.exp(-jnp.square((radius_sq[:, None] - centres[None, :]) / RADIAL_WIDTH))
    embed_first = jnp.dot(onehot_first, species_embed, precision=lax.Precision.HIGHEST)
    embed_second = jnp.dot(onehot_second, species_embed, precision=lax.Precision.HIGHEST)
    features = jnp.concatenate([radial, embed_first + embed_second, embed_first * embed_second], axis=1).astype(jnp.bfloat16)
    hidden = jax.nn.silu(jnp.dot(features, w_latent, preferred_element_type=jnp.float32))
    hidden_low = hidden.astype(jnp.bfloat16)
    weights = jnp.dot(hidden_low, w_channel, preferred_element_type=jnp.float32) * jnp.exp(-0.5 * radius_sq)[:, None]
    return (hidden_low, weights)

def pair_tensors(displace, weights):
    row_count = weights.shape[0]
    channels = weights.shape[1] // 3
    solid = harmonics(displace)
    per_component = weights.reshape(row_count, 3, channels)[:, DEGREE, :]
    tensor_first = (per_component * solid[:, :, None]).reshape(row_count, 9 * channels)
    tensor_second = (per_component * (solid * PARITY)[:, :, None]).reshape(row_count, 9 * channels)
    return (tensor_first, tensor_second)

def pair_env(displace, onehot_first, onehot_second, valid_mask, species_embed, w_latent, w_channel):
    hidden_low, weights = pair_latent(displace, onehot_first, onehot_second, species_embed, w_latent, w_channel)
    tensor_first, tensor_second = pair_tensors(displace, weights)
    pair_scale = ENV_SCALE * valid_mask[:, None]
    return (pair_scale * tensor_first, pair_scale * tensor_second)

def invariants(tensor, environ):
    row_count = tensor.shape[0]
    channels = tensor.shape[1] // 9
    product = (tensor * environ).reshape(row_count, 9, channels)
    return jnp.concatenate([product[:, 0], lax.optimization_barrier(jnp.sum(product[:, 1:4], axis=1)), lax.optimization_barrier(jnp.sum(product[:, 4:9], axis=1))], axis=1)

def pair_energy(displace, onehot_first, onehot_second, env_first, env_second, valid_mask, species_embed, w_latent, w_channel, w_energy, w_invariant, energy_vector):
    hidden_low, weights = pair_latent(displace, onehot_first, onehot_second, species_embed, w_latent, w_channel)
    tensor_first, tensor_second = pair_tensors(displace, weights)
    shared = jnp.dot(hidden_low, w_energy, preferred_element_type=jnp.float32)

    def centre(tensor, environ):
        inv_low = invariants(tensor, environ).astype(jnp.bfloat16)
        active = jax.nn.silu(shared + jnp.dot(inv_low, w_invariant, preferred_element_type=jnp.float32))
        return jnp.dot(active, energy_vector, precision=lax.Precision.HIGHEST)
    return jnp.sum(valid_mask * (centre(tensor_first, env_first) + centre(tensor_second, env_second)))

def reference(positions, species, send_list, pair_first, pair_second, species_embed, w_latent, w_channel, w_energy, w_invariant, energy_vector):
    devices = N_GX * N_GY * N_GZ
    atom_count = ATOM_DEV
    total_atoms = devices * atom_count
    float_type = positions.dtype
    width = 9 * species_embed.shape[1]
    device_grid = jnp.arange(devices, dtype=jnp.int32).reshape(N_GX, N_GY, N_GZ)
    ghost_blocks = []
    for slot_index in range(27):
        roll_shift = (1 - slot_index // 9, 1 - slot_index // 3 % 3, 1 - slot_index % 3)
        source_list = jnp.roll(send_list[:, :, :, 26 - slot_index, :], roll_shift, axis=(0, 1, 2))
        source_device = jnp.roll(device_grid, roll_shift, axis=(0, 1, 2))
        ghost_blocks.append(jnp.where(source_list >= 0, source_device[..., None] * atom_count + source_list, total_atoms))
    ghost_ids = jnp.stack(ghost_blocks, axis=3).reshape(devices, 27 * GHOSTS)
    own_ids = jnp.arange(total_atoms, dtype=jnp.int32).reshape(devices, atom_count)
    table_ids = jnp.concatenate([own_ids, ghost_ids], axis=1).astype(jnp.int32)
    slot_offsets = np.array([[slot_index // 9 - 1, slot_index // 3 % 3 - 1, slot_index % 3 - 1] for slot_index in range(27)], dtype=np.float32)
    table_shift = jnp.asarray(np.concatenate([np.zeros((atom_count, 3), dtype=np.float32), np.repeat(slot_offsets, GHOSTS, axis=0)], axis=0), dtype=float_type)
    flat_pos = jnp.concatenate([positions.reshape(total_atoms, 3), jnp.zeros((1, 3), float_type)], axis=0)
    flat_onehot = jnp.concatenate([jax.nn.one_hot(species.reshape(total_atoms), NSPEC, dtype=float_type), jnp.zeros((1, NSPEC), float_type)], axis=0)
    firsts = pair_first.reshape(devices, PAIRS_DEV).astype(jnp.int32)
    seconds_raw = pair_second.reshape(devices, PAIRS_DEV).astype(jnp.int32)
    seconds = jnp.maximum(seconds_raw, 0)
    valid_all = (seconds_raw >= 0).astype(float_type)
    scanned = (table_ids, firsts, seconds, valid_all)

    def geometry(row_ids, first_rows, second_rows):
        atom_pos = flat_pos[row_ids] + table_shift
        atom_onehot = flat_onehot[row_ids]
        displace = atom_pos[second_rows] - atom_pos[first_rows]
        return (displace, atom_onehot[first_rows], atom_onehot[second_rows])

    def env_step(env_sum, inputs):
        row_ids, first_rows, second_rows, valid_mask = inputs
        displace, onehot_first, onehot_second = geometry(row_ids, first_rows, second_rows)
        part_first, part_second = pair_env(displace, onehot_first, onehot_second, valid_mask, species_embed, w_latent, w_channel)
        env_sum = env_sum.at[row_ids[first_rows]].add(part_first)
        env_sum = env_sum.at[row_ids[second_rows]].add(part_second)
        return (env_sum, None)
    env_total, unused_out = lax.scan(env_step, jnp.zeros((total_atoms + 1, width), float_type), scanned)

    def energy_step(totals, inputs):
        energy_sum, grad_pos, grad_env = totals
        row_ids, first_rows, second_rows, valid_mask = inputs
        displace, onehot_first, onehot_second = geometry(row_ids, first_rows, second_rows)
        env_rows = env_total[row_ids]

        def block_energy(displace_in, env_first, env_second):
            return pair_energy(displace_in, onehot_first, onehot_second, env_first, env_second, valid_mask, species_embed, w_latent, w_channel, w_energy, w_invariant, energy_vector)
        energy_part, pullback = jax.vjp(block_energy, displace, env_rows[first_rows], env_rows[second_rows])
        grad_disp, grad_first, grad_second = pullback(jnp.ones_like(energy_part))
        grad_pos = grad_pos.at[row_ids[first_rows]].add(-grad_disp).at[row_ids[second_rows]].add(grad_disp)
        grad_env = grad_env.at[row_ids[first_rows]].add(grad_first).at[row_ids[second_rows]].add(grad_second)
        return ((energy_sum + energy_part, grad_pos, grad_env), None)
    start_totals = (jnp.zeros((), float_type), jnp.zeros((total_atoms + 1, 3), float_type), jnp.zeros((total_atoms + 1, width), float_type))
    (energy_sum, grad_pos, grad_env), unused_out = lax.scan(energy_step, start_totals, scanned)

    def force_step(grad_pos, inputs):
        row_ids, first_rows, second_rows, valid_mask = inputs
        displace, onehot_first, onehot_second = geometry(row_ids, first_rows, second_rows)
        adjoint_rows = grad_env[row_ids]

        def block_env(displace_in):
            return pair_env(displace_in, onehot_first, onehot_second, valid_mask, species_embed, w_latent, w_channel)
        unused_env, pullback = jax.vjp(block_env, displace)
        grad_disp, = pullback((adjoint_rows[first_rows], adjoint_rows[second_rows]))
        grad_pos = grad_pos.at[row_ids[first_rows]].add(-grad_disp).at[row_ids[second_rows]].add(grad_disp)
        return (grad_pos, None)
    grad_pos, unused_out = lax.scan(force_step, grad_pos, scanned)
    forces = -grad_pos[:total_atoms].reshape(N_GX, N_GY, N_GZ, atom_count, 3)
    return (forces, (energy_sum / total_atoms).reshape(1))
```

```python
import math

import jax
import jax.numpy as jnp
import numpy as np
from jax import lax
from jax.experimental import pallas as pl
from jax.experimental.layout import Layout, with_layout_constraint
from jax.experimental.pallas import tpu as pltpu
from jax.sharding import PartitionSpec as P

BLOCK = 256


DEGREE = np.array([0, 1, 1, 1, 2, 2, 2, 2, 2])
PARITY = np.array([1.0, -1.0, -1.0, -1.0, 1.0, 1.0, 1.0, 1.0, 1.0], dtype=np.float32)
ENV_SCALE = 0.1
RADIAL_STEP = 0.5
RADIAL_WIDTH = 0.35
ROOT_THREE = math.sqrt(3.0)
ROOT_FIVE = math.sqrt(5.0)
ROOT_FIFTEEN = math.sqrt(15.0)


def extended(cells, sides, width):
    for axis, dim in sides:
        count = lax.axis_size(axis)
        head = lax.slice_in_dim(cells, 0, width, axis=dim)
        tail = lax.slice_in_dim(cells, cells.shape[dim] - width, cells.shape[dim], axis=dim)
        cells = jnp.concatenate(
            [
                lax.ppermute(tail, axis, [(i, (i + 1) % count) for i in range(count)]),
                cells,
                lax.ppermute(head, axis, [((i + 1) % count, i) for i in range(count)]),
            ],
            axis=dim,
        )
    return cells


def harmonics(displace):
    coord_x = displace[:, 0]
    coord_y = displace[:, 1]
    coord_z = displace[:, 2]
    radius_sq = coord_x * coord_x + coord_y * coord_y + coord_z * coord_z
    return jnp.stack(
        [
            jnp.ones_like(coord_x),
            ROOT_THREE * coord_x,
            ROOT_THREE * coord_y,
            ROOT_THREE * coord_z,
            ROOT_FIFTEEN * coord_x * coord_y,
            ROOT_FIFTEEN * coord_y * coord_z,
            0.5 * ROOT_FIVE * (3.0 * coord_z * coord_z - radius_sq),
            ROOT_FIFTEEN * coord_x * coord_z,
            0.5 * ROOT_FIFTEEN * (coord_x * coord_x - coord_y * coord_y),
        ],
        axis=1,
    )


def pair_latent(displace, onehot_first, onehot_second, species_embed, w_latent, w_channel):
    radius_sq = jnp.sum(displace * displace, axis=1)
    basis_count = w_latent.shape[0] - 2 * species_embed.shape[1]
    centres = RADIAL_STEP * jnp.arange(basis_count).astype(displace.dtype)
    radial = jnp.exp(-jnp.square((radius_sq[:, None] - centres[None, :]) / RADIAL_WIDTH))
    embed_first = jnp.dot(onehot_first, species_embed, precision=lax.Precision.HIGHEST)
    embed_second = jnp.dot(onehot_second, species_embed, precision=lax.Precision.HIGHEST)
    features = jnp.concatenate(
        [radial, embed_first + embed_second, embed_first * embed_second], axis=1
    ).astype(jnp.bfloat16)
    hidden = jax.nn.silu(jnp.dot(features, w_latent, preferred_element_type=jnp.float32))
    hidden_low = hidden.astype(jnp.bfloat16)
    weights = (
        jnp.dot(hidden_low, w_channel, preferred_element_type=jnp.float32)
        * jnp.exp(-0.5 * radius_sq)[:, None]
    )
    return (hidden_low, weights)


def pair_tensors(displace, weights):
    row_count = weights.shape[0]
    channels = weights.shape[1] // 3
    solid = harmonics(displace)
    per_component = weights.reshape(row_count, 3, channels)[:, DEGREE, :]
    tensor_first = (per_component * solid[:, :, None]).reshape(row_count, 9 * channels)
    tensor_second = (per_component * (solid * PARITY)[:, :, None]).reshape(row_count, 9 * channels)
    return (tensor_first, tensor_second)


def pair_env(displace, onehot_first, onehot_second, valid_mask, species_embed, w_latent, w_channel):
    hidden_low, weights = pair_latent(
        displace, onehot_first, onehot_second, species_embed, w_latent, w_channel
    )
    tensor_first, tensor_second = pair_tensors(displace, weights)
    pair_scale = ENV_SCALE * valid_mask[:, None]
    return (pair_scale * tensor_first, pair_scale * tensor_second)


def invariants(tensor, environ):
    row_count = tensor.shape[0]
    channels = tensor.shape[1] // 9
    product = (tensor * environ).reshape(row_count, 9, channels)
    return jnp.concatenate(
        [product[:, 0], jnp.sum(product[:, 1:4], axis=1), jnp.sum(product[:, 4:9], axis=1)], axis=1
    )


def pair_energy(
    displace,
    onehot_first,
    onehot_second,
    env_first,
    env_second,
    valid_mask,
    species_embed,
    w_latent,
    w_channel,
    w_energy,
    w_invariant,
    energy_vector,
):
    hidden_low, weights = pair_latent(
        displace, onehot_first, onehot_second, species_embed, w_latent, w_channel
    )
    tensor_first, tensor_second = pair_tensors(displace, weights)
    shared = jnp.dot(hidden_low, w_energy, preferred_element_type=jnp.float32)

    def centre(tensor, environ):
        inv_low = invariants(tensor, environ).astype(jnp.bfloat16)
        active = jax.nn.silu(
            shared + jnp.dot(inv_low, w_invariant, preferred_element_type=jnp.float32)
        )
        return jnp.dot(active, energy_vector, precision=lax.Precision.HIGHEST)

    return jnp.sum(
        valid_mask * (centre(tensor_first, env_first) + centre(tensor_second, env_second))
    )


def trade(outgoing):
    padded = extended(outgoing, (("gx", 0), ("gy", 1), ("gz", 2)), 1)
    return padded[::2, ::2, ::2]


def general(
    positions,
    species,
    send_list,
    pair_first,
    pair_second,
    species_embed,
    w_latent,
    w_channel,
    w_energy,
    w_invariant,
    energy_vector,
):
    own_pos = positions.reshape(-1, 3)
    atom_count = own_pos.shape[0]
    sends = send_list.reshape(27, -1)
    ghost_slots = sends.shape[1]
    ghost_total = 27 * ghost_slots
    row_total = atom_count + ghost_total
    width = 9 * species_embed.shape[1]
    present = (sends >= 0).reshape(-1, 1).astype(jnp.float32)
    send_rows = jnp.maximum(sends, 0).reshape(-1)
    return_rows = jnp.where(sends >= 0, sends, atom_count).reshape(-1)
    slot_offsets = np.array(
        [
            [slot_index // 9 - 1, slot_index // 3 % 3 - 1, slot_index % 3 - 1]
            for slot_index in range(27)
        ],
        dtype=np.float32,
    )
    ghost_shift = jnp.asarray(np.repeat(slot_offsets, ghost_slots, axis=0))

    def forward(own_rows):
        columns = own_rows.shape[1]
        outgoing = (jnp.take(own_rows, send_rows, axis=0) * present).reshape(
            3, 3, 3, ghost_slots, columns
        )
        return trade(outgoing).reshape(ghost_total, columns)

    def backward(table_rows):
        columns = table_rows.shape[1]
        incoming = trade(table_rows[atom_count:].reshape(3, 3, 3, ghost_slots, columns))
        return (
            table_rows[:atom_count]
            .at[return_rows]
            .add(incoming.reshape(ghost_total, columns), mode="drop")
        )

    own_onehot = jax.nn.one_hot(species.reshape(-1), species_embed.shape[0], dtype=jnp.float32)
    ghost_data = forward(jnp.concatenate([own_pos, own_onehot], axis=1))
    table_pos = jnp.concatenate([own_pos, ghost_data[:, :3] + ghost_shift], axis=0)
    table_onehot = jnp.concatenate([own_onehot, ghost_data[:, 3:]], axis=0)
    firsts_all = pair_first.reshape(-1)
    seconds_all = pair_second.reshape(-1)
    used_blocks = (jnp.sum((seconds_all >= 0).astype(jnp.int32)) + BLOCK - 1) // BLOCK

    def block_pairs(block_index):
        offset_rows = block_index * BLOCK
        first_rows = lax.dynamic_slice_in_dim(firsts_all, offset_rows, BLOCK)
        second_raw = lax.dynamic_slice_in_dim(seconds_all, offset_rows, BLOCK)
        valid_mask = (second_raw >= 0).astype(jnp.float32)
        second_rows = jnp.maximum(second_raw, 0)
        displace = table_pos[second_rows] - table_pos[first_rows]
        return (first_rows, second_rows, valid_mask, displace)

    def env_block(block_index, env_part):
        first_rows, second_rows, valid_mask, displace = block_pairs(block_index)
        part_first, part_second = pair_env(
            displace,
            table_onehot[first_rows],
            table_onehot[second_rows],
            valid_mask,
            species_embed,
            w_latent,
            w_channel,
        )
        return env_part.at[first_rows].add(part_first).at[second_rows].add(part_second)

    env_part = lax.fori_loop(0, used_blocks, env_block, jnp.zeros((row_total, width), jnp.float32))
    env_own = backward(env_part)
    table_env = jnp.concatenate([env_own, forward(env_own)], axis=0)

    def energy_block(block_index, totals):
        energy_sum, grad_pos, grad_env = totals
        first_rows, second_rows, valid_mask, displace = block_pairs(block_index)
        onehot_first = table_onehot[first_rows]
        onehot_second = table_onehot[second_rows]

        def block_energy(displace_in, env_first, env_second):
            return pair_energy(
                displace_in,
                onehot_first,
                onehot_second,
                env_first,
                env_second,
                valid_mask,
                species_embed,
                w_latent,
                w_channel,
                w_energy,
                w_invariant,
                energy_vector,
            )

        energy_part, pullback = jax.vjp(
            block_energy, displace, table_env[first_rows], table_env[second_rows]
        )
        grad_disp, grad_first, grad_second = pullback(jnp.ones_like(energy_part))
        grad_pos = grad_pos.at[first_rows].add(-grad_disp).at[second_rows].add(grad_disp)
        grad_env = grad_env.at[first_rows].add(grad_first).at[second_rows].add(grad_second)
        return (energy_sum + energy_part, grad_pos, grad_env)

    start_totals = (
        jnp.zeros((), jnp.float32),
        jnp.zeros((row_total, 3), jnp.float32),
        jnp.zeros((row_total, width), jnp.float32),
    )
    energy_sum, grad_pos, grad_env = lax.fori_loop(0, used_blocks, energy_block, start_totals)
    adjoint_own = backward(grad_env)
    table_adjoint = jnp.concatenate([adjoint_own, forward(adjoint_own)], axis=0)

    def force_block(block_index, grad_pos):
        first_rows, second_rows, valid_mask, displace = block_pairs(block_index)
        onehot_first = table_onehot[first_rows]
        onehot_second = table_onehot[second_rows]

        def block_env(displace_in):
            return pair_env(
                displace_in,
                onehot_first,
                onehot_second,
                valid_mask,
                species_embed,
                w_latent,
                w_channel,
            )

        unused_env, pullback = jax.vjp(block_env, displace)
        (grad_disp,) = pullback((table_adjoint[first_rows], table_adjoint[second_rows]))
        return grad_pos.at[first_rows].add(-grad_disp).at[second_rows].add(grad_disp)

    grad_pos = lax.fori_loop(0, used_blocks, force_block, grad_pos)
    forces = -backward(grad_pos)
    grand_total = lax.psum(energy_sum, ("gx", "gy", "gz"))
    atoms_all = atom_count * lax.axis_size("gx") * lax.axis_size("gy") * lax.axis_size("gz")
    return (forces.reshape(positions.shape), (grand_total / atoms_all).reshape(1))


PACK = 256
PART = 3
CHUNK = PART * 128
ATOMS = 128
SLOTS = 27
GHOSTS = 8
LANES = 128
CAP = LANES - GHOSTS
HERE = 13
SIDE_ROWS = 9 * 8
OWN_TILES = 16
GROUPS = 32
MASKED = 10
C = 64
WIDTH = 9 * C
NB = 8
NSPEC = 5
COMBOS = 32
OWN_CHUNKS = -(-OWN_TILES // PART)
EDGE_CHUNKS = -(-42 // PART)
CHUNKS = OWN_CHUNKS + EDGE_CHUNKS
EDGE_START = OWN_CHUNKS * PART

R3, R5, R15 = ROOT_THREE, ROOT_FIVE, ROOT_FIFTEEN

LEVEL = (0, 2, 2, 2, 2, 2, 1, 1, 1)
EVEN = 6 * C

F32 = jnp.float32
BF16 = jnp.bfloat16
NN = (((1,), (0,)), ((), ()))
NT = (((1,), (1,)), ((), ()))
TN = (((0,), (0,)), ((), ()))


def mm(a, b, dims=NN):
    return lax.dot_general(a, b, dims, preferred_element_type=F32)


def split2(x):
    hi = x.astype(BF16)
    return hi, (x - hi.astype(F32)).astype(BF16)


def split3(x):
    hi = x.astype(BF16).astype(F32)
    mid = (x - hi).astype(BF16).astype(F32)
    return hi, mid, x - hi - mid


def iota(shape, axis):
    return lax.broadcasted_iota(jnp.int32, shape, axis)


def one_hot(index, rows):
    return (iota((rows, index.shape[1]), 0) == index).astype(F32)


def solids(x, y, z, r2):
    return (
        None,
        R15 * x * y,
        R15 * y * z,
        0.5 * R5 * (3.0 * z * z - r2),
        R15 * x * z,
        0.5 * R15 * (x * x - y * y),
        R3 * x,
        R3 * y,
        R3 * z,
    )


def scaled(block, solid):
    return block if solid is None else block * solid


def block_of(array, k):
    return array[k * C : (k + 1) * C]


def own_table(positions_ref, species_ref):
    return jnp.concatenate(
        [
            positions_ref[0],
            positions_ref[1],
            positions_ref[2],
            species_ref[...].astype(F32),
            jnp.zeros((4, ATOMS), F32),
        ],
        axis=0,
    )


def rows_of(own, atoms):
    return jnp.concatenate(
        [
            jnp.take_along_axis(
                own,
                jnp.broadcast_to(atoms[:, at : at + LANES], (8, LANES)),
                axis=1,
                mode="promise_in_bounds",
            )
            for at in range(0, atoms.shape[1], LANES)
        ],
        axis=1,
    )


def pair_rows(vector, kind, column, first):
    hi, mid, low = split3(vector)
    one = jnp.ones_like(kind)
    zero = jnp.zeros_like(kind)
    parts = [hi[0:3], kind, column, first, one, zero, mid[0:3], zero, low[0:3], zero]
    return jnp.concatenate(parts, axis=0)


def from_terms(total_ref, t):
    upper = total_ref[t * 16 : t * 16 + 8, :]
    lower = total_ref[t * 16 + 8 : t * 16 + 16, :]
    return upper + jnp.where(iota((8, LANES), 0) < 3, lower + pltpu.roll(lower, 4, 0), 0.0)


def sixteen_rows(tiles, groups):
    return ((iota((16 * tiles, groups), 0) >> 4) == iota((16 * tiles, groups), 1)).astype(
        F32
    ).astype(BF16)


def earlier_lanes():
    return (iota((PACK, PACK), 0) < iota((PACK, PACK), 1)).astype(BF16)


def pack_kernel(
    positions_ref,
    species_ref,
    sends_ref,
    first_ref,
    second_ref,
    low_ref,
    mid_ref,
    high_ref,
    over_ref,
    total_ref,
    picked_ref,
    lane_ref,
):
    row = iota((8, LANES), 0)
    lanes = iota((8, LANES), 1)
    own = own_table(positions_ref, species_ref)
    earlier = earlier_lanes()
    tiles = [s for s in range(SLOTS) if s != HERE]
    rows = sixteen_rows(MASKED, GROUPS)
    count = jnp.zeros((GROUPS, 1), F32)
    for start in range(0, second_ref.shape[1], PACK):
        first = first_ref[:, start : start + PACK]
        ghost = second_ref[:, start : start + PACK] - ATOMS
        near = rows_of(own, first)
        slot = ghost >> 3
        group = jnp.where(ghost >= 0, jnp.where(slot > HERE, slot - 1, slot), -1)
        member = one_hot(group, GROUPS)
        low_member = member.astype(BF16)
        rank = mm(low_member, earlier) + count
        rank = jnp.sum(rank * member, axis=0, keepdims=True).astype(jnp.int32)
        count = count + jnp.sum(member, axis=1, keepdims=True)
        lane = jnp.where(rank < CAP, rank, -1)
        column = (ghost & 7).astype(F32)
        data = pair_rows(near, near[3:4], column, first.astype(F32))
        here = slice(start, start + PACK)
        picked = mm(rows, low_member) * jnp.concatenate([data] * MASKED, axis=0)
        picked_ref[: 16 * MASKED, here] = picked.astype(BF16)
        low = data.astype(BF16)
        for t in range(MASKED, len(tiles)):
            picked = jnp.where(group == t, low, jnp.zeros_like(low))
            picked_ref[16 * t : 16 * t + 16, here] = picked
        lane_ref[:, here] = one_hot(lane, LANES).astype(BF16)
    total_ref[...] = mm(picked_ref[...], lane_ref[...], NT)
    spread = (iota((GHOSTS, LANES), 1) == iota((GHOSTS, LANES), 0) + CAP).astype(BF16)
    atoms = mm(sends_ref[...].astype(F32).astype(BF16), spread, TN).astype(jnp.int32)
    for s in range(SLOTS):
        ref = (low_ref, mid_ref, high_ref)[s // 9]
        if s == HERE:
            tile = jnp.zeros((8, LANES), F32)
        else:
            listed = atoms[s : s + 1]
            ghosts = rows_of(own, jnp.maximum(listed, 0))
            ghosts = jnp.where(row == 5, listed.astype(F32), ghosts)
            tile = jnp.where(lanes >= CAP, ghosts, from_terms(total_ref, tiles.index(s)))
        ref[s % 9 * 8 : s % 9 * 8 + 8, :] = tile
    crowded = (count > CAP).astype(F32)
    over_ref[...] = jnp.zeros((8, LANES), F32) + jnp.sum(crowded, axis=0, keepdims=True)


def inner_kernel(positions_ref, species_ref, first_ref, second_ref, pairs_ref, total_ref):
    own = own_table(positions_ref, species_ref)
    earlier = earlier_lanes()
    tiles = range(OWN_TILES)
    count = jnp.zeros((8, 1), F32)
    for start in range(0, second_ref.shape[1], PACK):
        first = first_ref[:, start : start + PACK]
        second = second_ref[:, start : start + PACK]
        inside = jnp.logical_and(second >= 0, second < ATOMS)
        near = rows_of(own, first)
        far = rows_of(own, jnp.clip(second, 0, ATOMS - 1))
        member = jnp.broadcast_to(inside.astype(F32), (8, PACK))
        rank = (mm(member.astype(BF16), earlier) + count)[0:1].astype(jnp.int32)
        count = count + jnp.sum(member, axis=1, keepdims=True)
        tile = jnp.where(inside, rank >> 7, -1)
        kind = near[3:4] * NSPEC + far[3:4]
        column = jnp.clip(second, 0, ATOMS - 1).astype(F32)
        data = pair_rows(far - near, kind, column, first.astype(F32))
        low = data.astype(BF16)
        picked = [jnp.where(tile == t, low, jnp.zeros_like(low)) for t in tiles]
        at_lane = one_hot(rank & 127, LANES).astype(BF16)
        part = mm(jnp.concatenate(picked, axis=0), at_lane, NT)
        if start == 0:
            total_ref[...] = part
        else:
            total_ref[...] += part
    for t in tiles:
        pairs_ref[t * 8 : t * 8 + 8, :] = from_terms(total_ref, t)


def whole_number(row):
    return jnp.sum(row, axis=1, keepdims=True).astype(jnp.int32)[0, 0]


def core_kernel(
    out_low_ref,
    out_mid_ref,
    out_high_ref,
    in_low_ref,
    in_mid_ref,
    in_high_ref,
    pairs_ref,
    over_ref,
    latent_ref,
    channel_ref,
    energy_w_ref,
    inv_w_ref,
    radial_w_ref,
    vector_ref,
    grad_own_ref,
    low_ref,
    mid_ref,
    high_ref,
    centre_ref,
    sum_ref,
    edge_ref,
    grad_ref,
    at_ref,
    slope_ref,
    weights_ref,
    hidden_ref,
    active_ref,
    grad_w_ref,
    grad_s_ref,
    total_ref,
    table_ref,
    env_ref,
    energy_ref,
    column_ref,
    energy_t_ref,
    inv_t_ref,
    shared_ref,
):
    row = iota((8, LANES), 0)
    lanes = iota((8, LANES), 1)

    spots = []
    filled = jnp.int32(0)
    sent_at = [
        (out_low_ref, out_mid_ref, out_high_ref)[s // 9][s % 9 * 8 : s % 9 * 8 + 8, :]
        for s in range(SLOTS)
    ]
    got_at = [
        (in_low_ref, in_mid_ref, in_high_ref)[s % 3][s // 3 * 8 : s // 3 * 8 + 8, :]
        for s in range(SLOTS)
    ]
    slots = [s for s in range(SLOTS) if s != HERE]
    centre_ref[2 * HERE : 2 * HERE + 2, :] = jnp.full((2, LANES), -1, jnp.int32)

    def at_column(table, column):
        index = jnp.broadcast_to(CAP + column.astype(jnp.int32), (8, LANES))
        return jnp.take_along_axis(table, index, axis=1, mode="promise_in_bounds")

    ghosts = [at_column(got_at[s], sent_at[s][4:5]) for s in slots]
    atoms = [at_column(sent_at[s], got_at[s][4:5]) for s in slots]
    tiles = []
    for s, ghost, atom in zip(slots, ghosts, atoms):
        sent, got = sent_at[s], got_at[s]
        offset = jnp.where(
            row == 0,
            float(s // 9 - 1),
            jnp.where(row == 1, float(s // 3 % 3 - 1), jnp.where(row == 2, float(s % 3 - 1), 0.0)),
        )
        ours = jnp.logical_and(lanes < CAP, sent[6:7] > 0.5)
        theirs = jnp.logical_and(lanes < CAP, got[6:7] > 0.5)
        tile = jnp.where(
            row < 3, (ghost + offset) - sent, jnp.where(row == 3, sent * NSPEC + ghost, sent)
        )
        tiles.append(jnp.where(ours, tile, 0.0))
        tile = jnp.where(
            row < 3,
            (got + offset) - atom,
            jnp.where(row == 3, got * NSPEC + atom, jnp.where(row == 5, atom, got)),
        )
        tiles.append(jnp.where(theirs, tile, 0.0))
    for k, tile in enumerate(tiles):
        at = 2 * slots[k // 2] + k % 2
        centre = jnp.where(tile[6:7] > 0.5, tile[5:6], -1.0)
        centre_ref[at : at + 1, :] = centre.astype(jnp.int32)
    counts = [jnp.sum(tile[6:7], axis=1, keepdims=True) for tile in tiles]
    counts = [count.astype(jnp.int32)[0, 0] for count in counts]
    held = jnp.zeros((8, LANES), F32)
    for tile, count in zip(tiles, counts):
        at = EDGE_START + (filled >> 7)
        shift = filled & 127
        turned = pltpu.roll(tile, shift, 1)
        whole = held + jnp.where(lanes >= shift, turned, 0.0)
        rest = jnp.where(lanes < shift, turned, 0.0)
        edge_ref[at] = whole
        edge_ref[at + 1] = rest
        held = jnp.where(shift + count >= LANES, rest, whole)
        spots.append((filled, count))
        filled = filled + count
    for k in range(1, PART + 1):
        edge_ref[EDGE_START + (filled >> 7) + k] = jnp.zeros((8, LANES), F32)
    for t in range(OWN_TILES, EDGE_START):
        edge_ref[t] = jnp.zeros((8, LANES), F32)
    own_count = jnp.zeros((1, LANES), F32)
    for t in range(OWN_TILES):
        tile = pairs_ref[t * 8 : t * 8 + 8, :]
        edge_ref[t] = tile
        own_count = own_count + tile[6:7]
    own_count = whole_number(own_count)
    own_chunks = (own_count + CHUNK - 1) // CHUNK
    edge_chunks = (filled + CHUNK - 1) // CHUNK
    column_ref[...] = jnp.transpose(jnp.broadcast_to(0.5 * vector_ref[...], (LANES, LANES)))
    energy_t_ref[...] = jnp.transpose(0.5 * energy_w_ref[...].astype(F32)).astype(BF16)
    inv_t_ref[...] = jnp.transpose(0.5 * inv_w_ref[...].astype(F32)).astype(BF16)

    def load(chunk):
        edges = jnp.concatenate([edge_ref[PART * chunk + k] for k in range(PART)], axis=1)
        x, y, z = edges[0:1], edges[1:2], edges[2:3]
        return edges, x, y, z, x * x + y * y + z * z, edges[6:7]

    def radial_of(r2):
        centre = RADIAL_STEP * iota((NB, 1), 0).astype(F32)
        shifted = (r2 - centre) * (1.0 / RADIAL_WIDTH)
        return centre, jnp.exp(-(shifted * shifted))

    def silu(half):
        bent = jnp.tanh(half)
        twice = bent + 1.0
        value = half * twice
        return value, twice + value * (1.0 - bent)

    def component(block, solid):
        return block if solid is None else block * solid.astype(BF16)

    def env_chunk(chunk, two, spare):
        edges, x, y, z, r2, valid = load(chunk)
        at_first = one_hot(jnp.where(valid > 0.5, edges[5:6], -1.0).astype(jnp.int32), ATOMS)
        at_ref[chunk, 0] = at_first.astype(BF16)
        if two:
            at_second = one_hot(jnp.where(valid > 0.5, edges[4:5], -1.0).astype(jnp.int32), ATOMS)
            even = (at_first + at_second).astype(BF16)
            odd = (at_first - at_second).astype(BF16)
            at_ref[chunk, 1] = at_second.astype(BF16)
            at_ref[chunk, 2] = even
            at_ref[chunk, 3] = odd
        else:
            even = odd = at_first.astype(BF16)
        combo = one_hot(edges[3:4].astype(jnp.int32), COMBOS)
        centre, radial = radial_of(r2)
        stacked = jnp.concatenate([combo, combo, radial, jnp.zeros_like(radial)], axis=0)
        half = mm(latent_ref[...], stacked.astype(BF16))
        yield
        hidden, active = silu(half)
        active_ref[chunk] = active
        hidden = hidden.astype(BF16)
        hidden_ref[chunk] = hidden
        weights = mm(channel_ref[...], hidden)
        yield
        weights = weights * jnp.exp(-0.5 * r2)
        weights_ref[chunk] = weights
        solid = solids(x, y, z, r2)
        weights = weights.astype(BF16)
        parts = [component(block_of(weights, LEVEL[m]), solid[m]) for m in range(9)]
        yield (jnp.concatenate(parts[:6], axis=0), even, jnp.concatenate(parts[6:], axis=0), odd)

    def energy_side(chunk, turned, two, spare, apart):
        edges, x, y, z, r2, valid = load(chunk)
        solid = solids(x, y, z, r2)
        solid = [-solid[m] if turned and LEVEL[m] == 1 else solid[m] for m in range(9)]
        at = at_ref[chunk, int(turned)]
        env_ref[spare] = mm(table_ref[...], at)
        shared = None if turned else mm(energy_t_ref[...], hidden_ref[chunk])
        if two and not turned:
            shared_ref[...] = shared
        yield
        weights = weights_ref[chunk]
        inner = [None] * 3
        for m in range(9):
            term = scaled(env_ref[spare, m * C : (m + 1) * C, :], solid[m])
            inner[LEVEL[m]] = term if inner[LEVEL[m]] is None else inner[LEVEL[m]] + term
        inner = jnp.concatenate(inner, axis=0)
        if turned:
            shared = shared_ref[...]
        half = shared + mm(inv_t_ref[...], (weights * inner).astype(BF16))
        yield
        act, slope = silu(half)
        energy_ref[...] += act * valid
        grad = jnp.concatenate([column_ref[...]] * (CHUNK // LANES), axis=1) * slope
        back = mm(inv_w_ref[...], grad.astype(BF16))
        yield
        back = back.astype(BF16).astype(F32)
        grad_w = back * inner
        up = back * weights
        slopes = []
        parts = []
        up_low = up.astype(BF16)
        for m in range(9):
            block = block_of(up, LEVEL[m])
            if m:
                slope = jnp.sum(block * env_ref[spare, m * C : (m + 1) * C, :], axis=0, keepdims=True)
                slopes.append(-slope if turned and LEVEL[m] == 1 else slope)
            parts.append(component(block_of(up_low, LEVEL[m]), solid[m]))
        slopes = jnp.concatenate(slopes, axis=0)
        if turned:
            grad_w_ref[chunk] += grad_w
            grad_s_ref[chunk] += grad
            slope_ref[chunk] += slopes
        else:
            grad_w_ref[chunk] = grad_w
            grad_s_ref[chunk] = grad
            slope_ref[chunk] = slopes
        parts = jnp.concatenate(parts, axis=0)
        if apart:
            total_ref[...] += mm(parts, at, NT)
        yield (parts, at)

    def force_chunk(chunk, two, spare):
        edges, x, y, z, r2, valid = load(chunk)
        solid = solids(x, y, z, r2)
        if two:
            env_ref[spare, :EVEN] = mm(table_ref[:EVEN], at_ref[chunk, 2])
            env_ref[spare, EVEN:] = mm(table_ref[EVEN:], at_ref[chunk, 3])
        else:
            env_ref[spare] = mm(table_ref[...], at_ref[chunk, 0])
        yield
        weights = weights_ref[chunk]
        grown = [None] * 3
        slopes = [None] * 9
        for m in range(9):
            level = LEVEL[m]
            block = env_ref[spare, m * C : (m + 1) * C, :]
            term = scaled(block, solid[m])
            grown[level] = term if grown[level] is None else grown[level] + term
            if m:
                slopes[m] = slope_ref[chunk, m - 1 : m, :] + jnp.sum(
                    block_of(weights, level) * block, axis=0, keepdims=True
                )
        grad_w = grad_w_ref[chunk] + jnp.concatenate(grown, axis=0)
        grad_r2 = -0.5 * jnp.sum(grad_w * weights, axis=0, keepdims=True)
        decay = jnp.exp(-0.5 * r2)
        back = mm(channel_ref[...], (grad_w * decay).astype(BF16), TN) + mm(
            energy_w_ref[...], grad_s_ref[chunk].astype(BF16)
        )
        yield
        back = back.astype(BF16).astype(F32) * active_ref[chunk]
        grad_radial = mm(radial_w_ref[...], back.astype(BF16))
        yield
        grad_radial = grad_radial[:NB].astype(BF16).astype(F32)
        centre, radial = radial_of(r2)
        grad_r2 += (-2.0 / RADIAL_WIDTH**2) * jnp.sum(
            grad_radial * radial * (r2 - centre), axis=0, keepdims=True
        )
        xy, yz, zz, xz, xx, px, py, pz = slopes[1:]
        grad_x = 2.0 * x * grad_r2 + R15 * (y * xy + z * xz + x * xx) - R5 * x * zz + R3 * px
        grad_y = 2.0 * y * grad_r2 + R15 * (x * xy + z * yz - y * xx) - R5 * y * zz + R3 * py
        grad_z = 2.0 * z * grad_r2 + R15 * (y * yz + x * xz) + 2.0 * R5 * z * zz + R3 * pz
        grads = jnp.concatenate([grad_x, grad_y, grad_z, jnp.zeros((5, CHUNK), F32)], axis=0)
        if not two:
            for k in range(PART):
                grad_ref[PART * chunk + k] = grads[:, k * LANES : (k + 1) * LANES]
        hi = grads.astype(BF16).astype(F32)
        parts = jnp.concatenate([hi, grads - hi], axis=0).astype(BF16)
        toward = at_ref[chunk, 3 if two else 0]
        yield (parts, toward)

    def together(works, lag=0):
        works = list(works)
        ends = [None] * len(works)
        turn = 0
        while None in ends:
            for k, work in enumerate(works):
                if turn >= lag * k and ends[k] is None:
                    ends[k] = next(work)
            turn += 1
        return ends

    def joined(parts):
        return parts[0] if len(parts) == 1 else jnp.concatenate(parts, axis=1)

    def env_step(items):
        ends = together(env_chunk(c, two, k) for k, (c, two) in enumerate(items))
        total_ref[:EVEN] += mm(joined([e[0] for e in ends]), joined([e[1] for e in ends]), NT)
        total_ref[EVEN:] += mm(joined([e[2] for e in ends]), joined([e[3] for e in ends]), NT)

    def energy_step(items):
        sides = []
        for c, two in items:
            sides.append((c, False, two))
            if two:
                sides.append((c, True, two))
        many = len(sides) > 2
        if many:
            sides = sides[2:] + sides[:2]
        ends = together(
            (energy_side(*side, k, many) for k, side in enumerate(sides)), int(many)
        )
        if not many:
            total_ref[...] += mm(joined([e[0] for e in ends]), joined([e[1] for e in ends]), NT)

    def force_step(items):
        ends = together(force_chunk(c, two, k) for k, (c, two) in enumerate(items))
        grad_own_ref[...] += mm(joined([e[0] for e in ends]), joined([e[1] for e in ends]), NT)

    def each(step):
        def both(chunk, carry):
            step([(chunk, True), (OWN_CHUNKS + chunk, False)])
            return carry

        def own(chunk, carry):
            step([(chunk, True)])
            return carry

        def outer(chunk, carry):
            step([(OWN_CHUNKS + chunk, False)])
            return carry

        def outer_two(pair, carry):
            chunk = OWN_CHUNKS + shared + 2 * pair
            step([(chunk, False), (chunk + 1, False)])
            return carry

        shared = jnp.minimum(own_chunks, edge_chunks)
        twos = (edge_chunks - shared) // 2
        lax.fori_loop(0, shared, both, 0)
        lax.fori_loop(shared, own_chunks, own, 0)
        lax.fori_loop(0, twos, outer_two, 0)
        lax.fori_loop(shared + 2 * twos, edge_chunks, outer, 0)

    total_ref[...] = jnp.zeros_like(total_ref)
    energy_ref[...] = jnp.zeros_like(energy_ref)
    grad_own_ref[...] = jnp.zeros_like(grad_own_ref)
    each(env_step)
    table_ref[...] = (ENV_SCALE * total_ref[...]).astype(BF16)
    total_ref[...] = jnp.zeros_like(total_ref)
    each(energy_step)
    table_ref[...] = (ENV_SCALE * total_ref[...]).astype(BF16)
    each(force_step)

    energy = sum(energy_ref[:, k * LANES : (k + 1) * LANES] for k in range(PART))
    energy = jnp.sum(2.0 * column_ref[...] * energy, axis=0, keepdims=True)
    energy = jnp.sum(energy, axis=1, keepdims=True)
    sums = jnp.where(lanes == 0, energy, over_ref[...])
    low_ref[SIDE_ROWS:, :] = sums
    high_ref[SIDE_ROWS:, :] = sums
    sum_ref[...] = sums

    def recall(spot):
        start, count = spot
        at = EDGE_START + (start >> 7)
        shift = start & 127
        tile = jnp.where(lanes >= shift, grad_ref[at], grad_ref[at + 1])
        return jnp.where(lanes < count, pltpu.roll(tile, (LANES - shift) & 127, 1), 0.0)

    place = 0
    for s in range(SLOTS):
        ref = (low_ref, mid_ref, high_ref)[s // 9]
        if s == HERE:
            tile = jnp.zeros((8, LANES), F32)
        else:
            tile = recall(spots[place]) + pltpu.roll(recall(spots[place + 1]), 4, 0)
            place += 2
        ref[s % 9 * 8 : s % 9 * 8 + 8, :] = tile


def final_kernel(own_ref, in_low_ref, in_mid_ref, in_high_ref, centre_ref, out_ref):
    total = -own_ref[...]
    for s in range(SLOTS):
        if s == HERE:
            continue
        ref = (in_low_ref, in_mid_ref, in_high_ref)[s % 3]
        tile = ref[s // 3 * 8 : s // 3 * 8 + 8, :]
        hi = tile.astype(BF16).astype(F32)
        parts = jnp.concatenate([hi, tile - hi], axis=0)
        theirs = one_hot(centre_ref[2 * s + 1 : 2 * s + 2, :], ATOMS)
        ours = one_hot(centre_ref[2 * s : 2 * s + 1, :], ATOMS)
        ats = jnp.concatenate([theirs, ours], axis=1).astype(BF16)
        both = jnp.concatenate([parts, pltpu.roll(parts, 12, 0)], axis=1).astype(BF16)
        total = total + mm(both, ats, NT)
    total = -(total[0:8] + total[8:16])
    for k in range(3):
        out_ref[k] = total[k : k + 1]


def shape(rows, cols, dtype=F32):
    return jax.ShapeDtypeStruct((rows, cols), dtype)


def shifted(cells, axis, step):
    count = lax.axis_size(axis)
    return lax.ppermute(cells, axis, [(i, (i + step) % count) for i in range(count)])


def settle(*arrays):
    return lax.optimization_barrier(arrays)


def swap_tiles(low, mid, high, sums=None, task=None):
    def pieces(left, mid, right, part):
        pick = slice(24 * part, 24 * part + 24)
        return [left[pick], mid[pick], right[pick]]

    row = lax.broadcasted_iota(jnp.int32, (8, LANES), 0)
    extra = [] if sums is None else [sums]
    left, right = shifted(high, "gx", 1), shifted(low, "gx", -1)
    if extra:
        even = lax.axis_index("gx") % 2 == 0
        sums = sums + jnp.where(even, left[SIDE_ROWS:], right[SIDE_ROWS:])
        extra = [sums]
    done = None
    if task is not None:
        run, arrays = task
        left, right, *arrays = settle(left, right, *arrays)
        done = run(*arrays)
    low, high = (
        jnp.concatenate(pieces(left, mid, right, part) + extra, axis=0) for part in (0, 2)
    )
    mid = jnp.concatenate(pieces(left, mid, right, 1), axis=0)
    left, right = shifted(high, "gy", 1), shifted(low, "gy", -1)
    if extra:
        far = shifted(sums, "gy", 2)
        left, right, far = settle(left, right, far)
        sums = sums + left[SIDE_ROWS:] + right[SIDE_ROWS:] + far
        extra = [sums]

    def tiles(part):
        picked = []
        for a in range(3):
            for array in (left, mid, right):
                start = 24 * a + 8 * part
                picked.append(array[start : start + 8])
        return picked

    low, high = (jnp.concatenate(tiles(part) + extra, axis=0) for part in (0, 2))
    mid = jnp.concatenate(tiles(1), axis=0)
    if task is not None:
        low, high, done = settle(low, high, done)
    left, right = shifted(high, "gz", 1), shifted(low, "gz", -1)
    if extra:
        before = left[SIDE_ROWS:]
        sums = sums + right[SIDE_ROWS:] + jnp.where(row % 2 == 0, before, 0.0)
    return left, mid, right, sums, done


def as_it_lies(array):
    return with_layout_constraint(array, Layout(major_to_minor=tuple(range(array.ndim))))


def grid_total(sums):
    sums = sums + shifted(sums, "gx", 4)
    sums = sums + other_core(sums)
    even = lax.axis_index("gx") % 2 == 0
    count_x, count_z = lax.axis_size("gx"), lax.axis_size("gz")
    moves = []
    for x in range(count_x):
        for z in range(count_z):
            to = (z + (3 if x % 2 else -3)) % count_z
            moves.append((x * count_z + z, x * count_z + to))
    rest = lax.ppermute(jnp.where(even, sums[0:1], sums[1:2]), ("gx", "gz"), moves)
    return sums[0:1] + rest + other_core(rest)


def other_core(array):
    return lax.ppermute(array, "gx", [(i, i ^ 1) for i in range(lax.axis_size("gx"))])


def per_device(
    positions,
    species,
    send_list,
    pair_first,
    pair_second,
    species_embed,
    w_latent,
    w_channel,
    w_energy,
    w_invariant,
    energy_vector,
):
    sides = (shape(SIDE_ROWS, LANES),) * 3
    small = pltpu.CompilerParams(vmem_limit_bytes=12 * 1024 * 1024)
    large = pltpu.CompilerParams(vmem_limit_bytes=48 * 1024 * 1024)
    places = positions.reshape(1, ATOMS, 3).transpose(2, 0, 1)
    kinds = species.reshape(1, ATOMS)
    sends = send_list.reshape(SLOTS, GHOSTS).T
    firsts = pair_first.reshape(1, -1)
    seconds = pair_second.reshape(1, -1)
    low, mid, high, over = pl.pallas_call(
        pack_kernel,
        out_shape=(*sides, shape(8, LANES)),
        scratch_shapes=[
            pltpu.VMEM(((SLOTS - 1) * 16, LANES), F32),
            pltpu.VMEM(((SLOTS - 1) * 16, seconds.shape[1]), BF16),
            pltpu.VMEM((LANES, seconds.shape[1]), BF16),
        ],
        compiler_params=small,
    )(places, kinds, sends, firsts, seconds)
    inner_call = pl.pallas_call(
        inner_kernel,
        out_shape=shape(OWN_TILES * 8, LANES),
        scratch_shapes=[pltpu.VMEM((OWN_TILES * 16, LANES), F32)],
        compiler_params=small,
    )
    in_low, in_mid, in_high, _, inner = swap_tiles(
        low, mid, high, task=(inner_call, (places, kinds, firsts, seconds))
    )

    embed_first = jnp.repeat(species_embed, NSPEC, axis=0)
    embed_second = jnp.tile(species_embed, (NSPEC, 1))
    features = jnp.concatenate(
        [embed_first + embed_second, embed_first * embed_second], axis=1
    ).astype(BF16)
    features = jnp.pad(features, ((0, COMBOS - NSPEC * NSPEC), (0, 0)))
    combos = mm(w_latent[NB:], features, (((0,), (1,)), ((), ())))
    high_part = lax.reduce_precision(combos, exponent_bits=8, mantissa_bits=7)
    hi, lo = high_part.astype(BF16), (combos - high_part).astype(BF16)
    radial_w = jnp.pad(0.5 * w_latent[:NB], ((0, 8), (0, 0)))
    latent_w = jnp.concatenate([0.5 * hi, 0.5 * lo, radial_w.T], axis=1)

    hidden_width, readout = w_energy.shape
    side = shape(SIDE_ROWS + 8, LANES)
    grad_own, low, mid, high, centres, sums = pl.pallas_call(
        core_kernel,
        out_shape=(
            shape(16, ATOMS),
            side,
            shape(SIDE_ROWS, LANES),
            side,
            shape(2 * SLOTS, LANES, jnp.int32),
            shape(8, LANES),
        ),
        scratch_shapes=[
            pltpu.VMEM((CHUNKS * PART + PART, 8, LANES), F32),
            pltpu.VMEM((CHUNKS * PART + PART, 8, LANES), F32),
            pltpu.VMEM((CHUNKS, 4, ATOMS, CHUNK), BF16),
            pltpu.VMEM((CHUNKS, 8, CHUNK), F32),
            pltpu.VMEM((CHUNKS, 3 * C, CHUNK), F32),
            pltpu.VMEM((CHUNKS, hidden_width, CHUNK), BF16),
            pltpu.VMEM((CHUNKS, hidden_width, CHUNK), F32),
            pltpu.VMEM((CHUNKS, 3 * C, CHUNK), F32),
            pltpu.VMEM((CHUNKS, readout, CHUNK), F32),
            pltpu.VMEM((WIDTH, ATOMS), F32),
            pltpu.VMEM((WIDTH, ATOMS), BF16),
            pltpu.VMEM((3, WIDTH, CHUNK), F32),
            pltpu.VMEM((readout, CHUNK), F32),
            pltpu.VMEM((readout, LANES), F32),
            pltpu.VMEM((readout, hidden_width), BF16),
            pltpu.VMEM((readout, 3 * C), BF16),
            pltpu.VMEM((readout, CHUNK), F32),
        ],
        compiler_params=large,
    )(
        low,
        mid,
        high,
        in_low,
        in_mid,
        in_high,
        inner,
        over,
        latent_w,
        w_channel.T,
        w_energy,
        w_invariant,
        radial_w,
        energy_vector.reshape(1, -1),
    )

    in_low, in_mid, in_high, sums, _ = swap_tiles(low, mid, high, sums)
    forces = pl.pallas_call(
        final_kernel,
        out_shape=jax.ShapeDtypeStruct((3, 1, ATOMS), F32),
        compiler_params=small,
    )(grad_own, in_low, in_mid, in_high, centres)
    sums = grid_total(sums)
    devices = lax.axis_size("gx") * lax.axis_size("gy") * lax.axis_size("gz")
    crowded = sums[0, 1] > 0.5
    energy = sums[0, :1] / (ATOMS * devices)

    def again(state):
        held = (places, kinds, sends, firsts, seconds, state[2])
        own_places, own_kinds, own_sends, own_firsts, own_seconds, _ = lax.optimization_barrier(held)
        own_places, own_sends = as_it_lies(own_places), as_it_lies(own_sends)
        forces, energy = general(
            own_places.transpose(1, 2, 0).reshape(positions.shape),
            own_kinds.reshape(species.shape),
            own_sends.T.reshape(send_list.shape),
            own_firsts.reshape(pair_first.shape),
            own_seconds.reshape(pair_second.shape),
            species_embed,
            w_latent,
            w_channel,
            w_energy,
            w_invariant,
            energy_vector,
        )
        forces = as_it_lies(forces.reshape(1, ATOMS, 3).transpose(2, 0, 1))
        return forces, energy, jnp.zeros((), bool)

    forces, energy, _ = lax.while_loop(lambda state: state[2], again, (forces, energy, crowded))
    return forces.transpose(1, 2, 0).reshape(positions.shape), energy


def solution(mesh):
    return jax.shard_map(
        per_device,
        mesh=mesh,
        in_specs=(
            P("gx", "gy", "gz", None, None),
            P("gx", "gy", "gz", None),
            P("gx", "gy", "gz", None, None),
            P("gx", "gy", "gz", None),
            P("gx", "gy", "gz", None),
            P(),
            P(),
            P(),
            P(),
            P(),
            P(),
        ),
        out_specs=(P("gx", "gy", "gz", None, None), P()),
        check_vma=False,
    )
```
